256 devices in a mesh: chan: 8 (over x, z_hi), seq: 32 (over z_lo, y, core).
Axes of the slice: x: 4, y: 4, z: 8 (z_hi: 2, z_lo: 4; z = z_hi * 4 + z_lo), core: 2. Of those that a mesh axis runs over, the one named last changes fastest.
Arguments:
- stream: bfloat16 [512, 1024, 512], P('seq', 'chan'), may hold values from -6 to 6
- weight_value: bfloat16 [512, 512], replicated, may hold values from -0.25 to 0.25
- weight_gate: bfloat16 [512, 512], replicated, may hold values from -0.25 to 0.25
- weight_out: bfloat16 [512, 512], replicated, may hold values from -0.25 to 0.25
- within_factor: bfloat16 [1024, 1024], replicated, may hold values from -0.1875 to 0.1875
- across_factor: bfloat16 [512, 512], replicated, may hold values from -0.25 to 0.25
- within_scale: bfloat16 [1024, 512], P(None, 'chan'), may hold values from -4 to 4
- across_scale: bfloat16 [512, 512], P(None, 'chan'), may hold values from -4 to 4
- mix_gain: bfloat16 [512], replicated, may hold values from 0.099609375 to 1.8984375
- final_gain: bfloat16 [512], replicated, may hold values from 0.099609375 to 1.8984375
- block_up: bfloat16 [4, 128, 512], replicated, may hold values from -0.5 to 0.5
- block_down: bfloat16 [4, 512, 128], replicated, may hold values from -0.25 to 0.25
Outputs:
- result: bfloat16 [512, 1024, 512], P('seq', 'chan')
The draws below stay inside these ranges and needn't reach their ends.
All inputs are finite; a program needn't handle non-finite values.
Results may differ from the reference program's by a relative error of at most 0.015.
Values may be sent and summed in bfloat16 or wider, within the bound.
A program may use at most 128 MiB of HBM per device.

```python
import jax
import jax.numpy as jnp
from jax import lax

A = 512
B = 1024
D = 512
HID = 2048
NBLK = 4


def level_of(own_key, dims, shards, least, high):
    def one(position, shards_of):
        draws = jax.random.uniform(jax.random.fold_in(jax.random.fold_in(own_key, 6), position), (shards_of,), jnp.float32, least / len(shards), high / len(shards))
        return jnp.repeat(jnp.exp(draws), dims[position] // shards_of).reshape((-1,) + (1,) * (len(dims) - position - 1))

    factor_of = one(*shards[0])
    for cut in shards[1:]:
        factor_of = factor_of * one(*cut)
    return factor_of


def scatter_about(rng, shape, spread, most, cuts=(), dtype=jnp.bfloat16):
    entries = spread * jax.random.normal(rng, shape, jnp.float32)
    if cuts:
        entries = entries * level_of(rng, shape, cuts, -0.22, 0.18)
    return jnp.clip(entries, -most, most).astype(dtype)


def setup_inputs(seed: int = 0) -> dict:
    splits = jax.random.split(jax.random.key(seed), 13)
    return {
        "stream": scatter_about(splits[0], (A, B, D), 1.0, 6.0, ((0, 32), (1, 8))),
        "weight_value": scatter_about(splits[1], (D, D), D ** -0.5, 0.25),
        "weight_gate": scatter_about(splits[2], (D, D), D ** -0.5, 0.25),
        "weight_out": scatter_about(splits[3], (D, D), D ** -0.5, 0.25),
        "within_factor": scatter_about(splits[4], (B, B), B ** -0.5, 0.1875),
        "across_factor": scatter_about(splits[5], (A, A), A ** -0.5, 0.25),
        "within_scale": scatter_about(splits[6], (B, D), 1.0, 4.0, ((1, 8),)),
        "across_scale": scatter_about(splits[7], (A, D), 1.0, 4.0, ((1, 8),)),
        "mix_gain": jnp.clip(1.0 + 0.18 * jax.random.normal(splits[8], (D,), jnp.float32), 0.099609375, 1.8984375).astype(jnp.bfloat16),
        "final_gain": jnp.clip(1.0 + 0.18 * jax.random.normal(splits[9], (D,), jnp.float32), 0.099609375, 1.8984375).astype(jnp.bfloat16),
        "block_up": scatter_about(splits[10], (NBLK, D // NBLK, HID // NBLK), (D // NBLK) ** -0.5, 0.5),
        "block_down": scatter_about(splits[11], (NBLK, HID // NBLK, D // NBLK), (HID // NBLK) ** -0.5, 0.25),
    }


eps = 1e-05
lane_group = 64
slab_rows = 16

def rms_scale(flat, gain):
    power = lax.optimization_barrier(jnp.mean(flat * flat, axis=-1, keepdims=True))
    return flat * lax.rsqrt(power + eps) * gain.astype(jnp.float32)

def reference(stream, weight_value, weight_gate, weight_out, within_factor, across_factor, within_scale, across_scale, mix_gain, final_gain, block_up, block_down):
    width = stream.shape[2]
    rows_b = stream.shape[1]
    rows_a = stream.shape[0]

    def front(rows):
        flat = rows.reshape(-1, width).astype(jnp.float32)
        normed = rms_scale(flat, mix_gain).astype(jnp.bfloat16)
        values = jnp.dot(normed, weight_value, preferred_element_type=jnp.float32).astype(jnp.bfloat16)
        gates = jnp.dot(normed, weight_gate, preferred_element_type=jnp.float32).astype(jnp.bfloat16)
        return (values.reshape(rows.shape), gates.reshape(rows.shape))
    values, gates = lax.map(front, stream.reshape(rows_a // slab_rows, slab_rows, rows_b, width))
    values = values.reshape(rows_a, rows_b, width)
    gates = gates.reshape(rows_a, rows_b, width)
    count = width // lane_group
    lower_within = jnp.tril(within_factor).astype(jnp.float32)
    lower_across = jnp.tril(across_factor).astype(jnp.float32)
    grouped = values.reshape(rows_a, rows_b, count, lane_group).transpose(2, 0, 1, 3)
    within_groups = within_scale.reshape(rows_b, count, lane_group).transpose(1, 0, 2)
    across_groups = across_scale.reshape(rows_a, count, lane_group).transpose(1, 0, 2)

    def mix(packed):
        piece, within_one, across_one = packed
        first = jnp.einsum('pb,abc->apc', lower_within, piece.astype(jnp.float32))
        first = (first * within_one.astype(jnp.float32)[None]).astype(jnp.bfloat16)
        second = jnp.einsum('qa,abc->qbc', lower_across, first.astype(jnp.float32))
        return (second * across_one.astype(jnp.float32)[:, None, :]).astype(jnp.bfloat16)
    mixed = lax.map(mix, (grouped, within_groups, across_groups))
    mixed = mixed.transpose(1, 2, 0, 3).reshape(rows_a, rows_b, width)
    mixed = lax.optimization_barrier(mixed)
    gated = (gates.astype(jnp.float32) * mixed.astype(jnp.float32)).astype(jnp.bfloat16)
    blocks = block_up.shape[0]

    def tail(packed):
        rows, gated_rows = packed
        flat = rows.reshape(-1, width).astype(jnp.float32)
        middle = (flat + jnp.dot(gated_rows.reshape(-1, width), weight_out, preferred_element_type=jnp.float32)).astype(jnp.bfloat16)
        renormed = rms_scale(middle.astype(jnp.float32), final_gain).astype(jnp.bfloat16)
        split = renormed.reshape(-1, blocks, width // blocks).astype(jnp.float32)
        inner = jax.nn.gelu(jnp.einsum('tkd,kdh->tkh', split, block_up.astype(jnp.float32)), approximate=True).astype(jnp.bfloat16)
        outer = jnp.einsum('tkh,khd->tkd', inner.astype(jnp.float32), block_down.astype(jnp.float32)).reshape(-1, width)
        return (middle.astype(jnp.float32) + outer).astype(jnp.bfloat16).reshape(rows.shape)
    shaped = (rows_a // slab_rows, slab_rows, rows_b, width)
    result = lax.map(tail, (stream.reshape(shaped), gated.reshape(shaped)))
    return result.reshape(rows_a, rows_b, width)
```

```python
import jax
import jax.numpy as jnp
from jax import lax
from jax.experimental import pallas as pl
from jax.experimental.pallas import tpu as pltpu
from jax.sharding import PartitionSpec as P

eps = 1e-05
MESH = pl.DeviceIdType.MESH
F32 = jnp.float32
BF16 = jnp.bfloat16
NX, NZ, NY, NC = 4, 8, 4, 2
LAST = (((1,), (1,)), ((), ()))
FIRST = (((0,), (0,)), ((), ()))


def dot(left, right, dims=None):
    if dims is None:
        return jnp.dot(left, right, preferred_element_type=F32)
    return lax.dot_general(left, right, dims, preferred_element_type=F32)


def rms(flat, gain):
    power = jnp.mean(flat * flat, axis=-1, keepdims=True)
    return flat * lax.rsqrt(power + eps) * gain


def gelu(h):
    cdf = 0.5 * (1.0 + jnp.tanh(0.7978845608028654 * (h + 0.044715 * (h * h * h))))
    return h * cdf


def place(x, z, y, core):
    return x * 2 + z // 4, (z % 4) * 8 + y * 2 + core


def kernel(
    stream_hbm, wv_hbm, wg_hbm, wo_hbm, within_hbm, across_hbm, ws_hbm, as_hbm,
    mix_hbm, final_hbm, up_hbm, down_hbm,
    out_hbm,
    stream, wv, wg, wo, within, across, ws, ascale, mix_gain, final_gain, up, down,
    wvt, wgt, wst, normed, gates,
    send1, recv1, send2, recv2, send3, recv3, flip1, flip2, result,
    in_sem, out_sem, s1, r1, s2, r2, s3, r3,
):
    chan = lax.axis_index("chan")
    seq = lax.axis_index("seq")
    x, z = chan // 2, (chan % 2) * 4 + seq // 8
    y, core = (seq // 2) % 4, seq % 2
    zl, yc = seq // 8, seq % 8
    own = x * 8 + z

    def p_block(half, y_of, core_of):
        return 2 * ((x + y_of + 2 * core_of + half) % NX) + core_of

    def load(number, source, target):
        return pltpu.make_async_copy(source, target, in_sem.at[number])

    loads = [
        load(0, stream_hbm, stream), load(1, wv_hbm, wv), load(2, mix_hbm, mix_gain),
        load(3, wg_hbm, wg), load(4, within_hbm, within), load(5, ws_hbm, ws),
        load(6, across_hbm, across), load(7, as_hbm, ascale), load(8, wo_hbm, wo),
        load(9, final_hbm, final_gain), load(10, up_hbm, up), load(11, down_hbm, down),
    ]
    for one in loads:
        one.start()

    barrier = pltpu.get_barrier_semaphore()

    def greet(x_of, z_of, y_of, core_of):
        pl.semaphore_signal(
            barrier, inc=1, device_id=place(x_of, z_of, y_of, core_of), device_id_type=MESH
        )

    @pl.loop(1, NX * NZ)
    def _(i):
        greet((x + i // NZ) % NX, (z + i % NZ) % NZ, y, core)

    @pl.loop(1, NY * NC)
    def _(i):
        greet(x, z, (y + i // NC) % NY, (core + i % NC) % NC)

    for half in range(2):
        @pl.loop(0, NX * NZ)
        def _(i):
            x_of = i // NZ
            core_of = chan % 2
            greet(x_of, i % NZ, (x - x_of - 2 * core_of - half + 2 * NX) % NY, core_of)

    for number in (1, 2):
        loads[number].wait()
    wvt[...] = wv[...].astype(F32).T.reshape(32, 2, 8, 512).swapaxes(0, 1).reshape(2, 256, 512).astype(BF16)
    loads[0].wait()
    gain = mix_gain[...].astype(F32)

    def values(half, pair, tokens):
        found = dot(wvt[half], tokens, LAST)
        split = [found[:, :128].reshape(32, 8, 128), found[:, 128:].reshape(32, 8, 128)]
        send1[half, :, pair] = jnp.concatenate(split, axis=1).astype(BF16)

    @pl.loop(0, 8)
    def _(pair):
        flat = stream[pl.ds(2 * pair, 2)].reshape(256, 512).astype(F32)
        tokens = rms(flat, gain).astype(BF16)
        normed[pair] = tokens
        values(0, pair, tokens)

    def send_values(half):
        pltpu.make_async_copy(send1.at[half, own], recv1.at[half, chan, zl], r1.at[half]).start()

        @pl.loop(1, NX * NZ)
        def _(i):
            x_of, z_of = (x + i // NZ) % NX, (z + i % NZ) % NZ
            pltpu.make_async_remote_copy(
                send1.at[half, x_of * 8 + z_of], recv1.at[half, chan, zl],
                s1.at[half], r1.at[half],
                device_id=place(x_of, z_of, y, core), device_id_type=MESH,
            ).start()

    pl.semaphore_wait(barrier, NX * NZ - 1 + NY * NC - 1 + 2 * NX * NZ)
    send_values(0)

    @pl.loop(0, 8)
    def _(pair):
        values(1, pair, normed[pair])

    send_values(1)

    loads[3].wait()
    wgt[...] = wg[...].astype(F32).T.astype(BF16)

    @pl.loop(0, 8)
    def _(pair):
        found = dot(wgt[...], normed[pair], LAST).astype(BF16)
        gates[2 * pair] = found[:, :128]
        gates[2 * pair + 1] = found[:, 128:]

    for number in range(4, 12):
        loads[number].wait()
    lower = lax.broadcasted_iota(jnp.int32, (256, 256), 0) >= lax.broadcasted_iota(jnp.int32, (256, 256), 1)
    for n in range(4):
        edge = pl.ds(256 * n, 256)
        within[edge, edge] = jnp.where(lower, within[edge, edge].astype(F32), 0.0).astype(BF16)
    for n in range(2):
        edge = pl.ds(256 * n, 256)
        across[edge, edge] = jnp.where(lower, across[edge, edge].astype(F32), 0.0).astype(BF16)
    picked = lax.broadcasted_iota(jnp.int32, (16, 64), 1) == 16 * zl + lax.broadcasted_iota(jnp.int32, (16, 64), 0)
    wst[...] = dot(picked.astype(F32).astype(BF16), ws[...], LAST)

    def middle_of(half):
        pltpu.make_async_copy(recv1.at[half], recv1.at[half], r1.at[half]).wait()
        for n in range(4):
            blocks = [recv1[half, k].reshape(512, 128) for k in range(2 * n + 2)]
            found = dot(
                jnp.concatenate(blocks, axis=1), within[pl.ds(256 * n, 256), pl.ds(0, 256 * (n + 1))], LAST
            )
            scale = wst[pl.ds(8 * half, 8), pl.ds(256 * n, 256)]
            scaled = (found.reshape(64, 8, 256) * scale[None]).reshape(512, 256)
            for side in range(2):
                flip1[side] = scaled[:, 128 * side : 128 * side + 128]
            for side in range(2):
                for c in range(8):
                    column = flip1[side, pl.ds(c, 64, stride=8), :]
                    send2[half, 2 * n + side, c] = column.astype(BF16).reshape(4, 16, 128)
        pltpu.make_async_copy(
            send2.at[half, p_block(half, y, core)], recv2.at[half, :, :, yc], r2.at[half]
        ).start()

        @pl.loop(1, NY * NC)
        def _(i):
            y_of, core_of = (y + i // NC) % NY, (core + i % NC) % NC
            pltpu.make_async_remote_copy(
                send2.at[half, p_block(half, y_of, core_of)], recv2.at[half, :, :, yc],
                s2.at[half], r2.at[half],
                device_id=place(x, z, y_of, core_of), device_id_type=MESH,
            ).start()

    def across_of(half):
        pltpu.make_async_copy(recv2.at[half], recv2.at[half], r2.at[half]).wait()
        for c in range(0, 8, 2):
            both = jnp.concatenate(
                [recv2[half, c].reshape(512, 128), recv2[half, c + 1].reshape(512, 128)], axis=1
            )
            row = lax.broadcasted_iota(jnp.int32, (64, 256), 0)
            wanted = 16 * zl + 8 * half + c + lax.broadcasted_iota(jnp.int32, (64, 256), 1) // 128
            spread = (row == wanted).astype(F32).astype(BF16)
            for n in range(2):
                rows = pl.ds(256 * n, 256)
                found = dot(across[rows, pl.ds(0, 256 * (n + 1))], both[: 256 * (n + 1)])
                found = found * dot(ascale[rows, :], spread)
                for side in range(2):
                    flip2[pl.ds(2048 * n + c + side, 256, stride=8), :] = found[:, 128 * side : 128 * side + 128]

        @pl.loop(0, 32)
        def _(block):
            start = pl.multiple_of(block * 128, 128)
            send3[half, block] = flip2[pl.ds(start, 128), :].reshape(8, 16, 128).astype(BF16)

    def send_mixed(half, first, count, sem):
        block = p_block(half, y, core)
        rows = pl.ds(first, count)

        def remote(i):
            zl_of, yc_of = (zl + i % 4) % 4, (yc + i // 4) % 8
            seq_of = zl_of * 8 + yc_of
            pltpu.make_async_remote_copy(
                send3.at[half, seq_of, rows], recv3.at[half, rows, own],
                s3.at[sem], r3.at[sem], device_id=(block, seq_of), device_id_type=MESH,
            ).start()

        @pl.when(block == chan)
        def _():
            pltpu.make_async_copy(
                send3.at[half, seq, rows], recv3.at[half, rows, own], r3.at[sem]
            ).start()

        @pl.when(block != chan)
        def _():
            remote(0)

        @pl.loop(1, 32)
        def _(i):
            remote(i)

    middle_of(0)
    across_of(0)
    send_mixed(0, 0, 8, 4)
    middle_of(1)
    across_of(1)
    for part in range(4):
        send_mixed(1, 2 * part, 2, part)

    pltpu.make_async_copy(recv3.at[0], recv3.at[0], r3.at[4]).wait()
    gain2 = final_gain[...].astype(F32)
    for part in range(4):
        arrived = recv3.at[1, pl.ds(2 * part, 2)]
        pltpu.make_async_copy(arrived, arrived, r3.at[part]).wait()

        @pl.loop(2 * part, 2 * part + 2)
        def _(pair):
            halves = [recv3[half, pair].astype(F32) for half in range(2)]
            projected = []
            for one in range(2):
                mixed = jnp.concatenate([h[:, 8 * one : 8 * one + 8] for h in halves], axis=1)
                gated = mixed.reshape(512, 128) * gates[2 * pair + one].astype(F32)
                projected.append(dot(gated.astype(BF16), wo[...], FIRST))
            flat = stream[pl.ds(2 * pair, 2)].reshape(256, 512).astype(F32)
            middle = (flat + jnp.concatenate(projected, axis=0)).astype(BF16).astype(F32)
            renormed = rms(middle, gain2).astype(BF16)
            outer = []
            for k in range(4):
                inner = gelu(dot(renormed[:, 128 * k : 128 * k + 128], up[k])).astype(BF16)
                outer.append(dot(inner, down[k]))
            total = (middle + jnp.concatenate(outer, axis=1)).astype(BF16)
            result[pl.ds(2 * pair, 2)] = total.reshape(2, 128, 512)

        rows = pl.ds(4 * part, 4)
        pltpu.make_async_copy(result.at[rows], out_hbm.at[rows], out_sem.at[part]).start()

    for half in range(2):
        sent = send1.at[half, pl.ds(0, 31)]
        pltpu.make_async_copy(sent, sent, s1.at[half]).wait()
        sent = send2.at[half, pl.ds(0, 7)]
        pltpu.make_async_copy(sent, sent, s2.at[half]).wait()
    for sem in range(5):
        rows = pl.ds(0, 8) if sem == 4 else pl.ds(2 * sem, 2)
        half = 0 if sem == 4 else 1
        rest = send3.at[half, pl.ds(1, 31), rows]
        pltpu.make_async_copy(rest, rest, s3.at[sem]).wait()

        @pl.when(p_block(half, y, core) != chan)
        def _():
            one = send3.at[half, 0, rows]
            pltpu.make_async_copy(one, one, s3.at[sem]).wait()

    for part in range(4):
        rows = pl.ds(4 * part, 4)
        pltpu.make_async_copy(result.at[rows], out_hbm.at[rows], out_sem.at[part]).wait()


def body(
    stream, weight_value, weight_gate, weight_out, within_factor, across_factor,
    within_scale, across_scale, mix_gain, final_gain, block_up, block_down,
):
    args = (
        stream, weight_value, weight_gate, weight_out, within_factor, across_factor,
        within_scale, across_scale, mix_gain.reshape(1, -1), final_gain.reshape(1, -1),
        block_up, block_down,
    )
    anywhere = pl.BlockSpec(memory_space=pl.ANY)
    return pl.pallas_call(
        kernel,
        out_shape=jax.ShapeDtypeStruct(stream.shape, BF16),
        in_specs=[anywhere] * len(args),
        out_specs=anywhere,
        scratch_shapes=[pltpu.VMEM(a.shape, BF16) for a in args] + [
            pltpu.VMEM((2, 256, 512), BF16),
            pltpu.VMEM((512, 512), BF16),
            pltpu.VMEM((16, 1024), F32),
            pltpu.VMEM((8, 256, 512), BF16),
            pltpu.VMEM((16, 512, 128), BF16),
            pltpu.VMEM((2, 32, 8, 16, 128), BF16),
            pltpu.VMEM((2, 8, 4, 8, 16, 128), BF16),
            pltpu.VMEM((2, 8, 8, 4, 16, 128), BF16),
            pltpu.VMEM((2, 8, 4, 8, 16, 128), BF16),
            pltpu.VMEM((2, 32, 8, 16, 128), BF16),
            pltpu.VMEM((2, 8, 32, 16, 128), BF16),
            pltpu.VMEM((2, 512, 128), F32),
            pltpu.VMEM((4096, 128), F32),
            pltpu.VMEM((16, 128, 512), BF16),
            pltpu.SemaphoreType.DMA((12,)),
            pltpu.SemaphoreType.DMA((4,)),
            pltpu.SemaphoreType.DMA((2,)),
            pltpu.SemaphoreType.DMA((2,)),
            pltpu.SemaphoreType.DMA((2,)),
            pltpu.SemaphoreType.DMA((2,)),
            pltpu.SemaphoreType.DMA((5,)),
            pltpu.SemaphoreType.DMA((5,)),
        ],
        compiler_params=pltpu.CompilerParams(
            collective_id=0, has_side_effects=True, vmem_limit_bytes=56 * 2**20
        ),
        cost_estimate=pl.CostEstimate(
            flops=9 * 10**9, bytes_accessed=12 * 2**20, transcendentals=2**22
        ),
        name="mixer",
    )(*args)


def solution(mesh):
    placed = (
        P("seq", "chan", None), P(), P(), P(), P(), P(), P(None, "chan"), P(None, "chan"),
        P(), P(), P(), P(),
    )
    return jax.shard_map(
        body, mesh=mesh, in_specs=placed, out_specs=P("seq", "chan", None), check_vma=False
    )
```

```python
import jax
import jax.numpy as jnp
from jax import lax
from jax.experimental import pallas as pl
from jax.experimental.pallas import tpu as pltpu
from jax.sharding import PartitionSpec as P

eps = 1e-05
MESH = pl.DeviceIdType.MESH
F32 = jnp.float32
BF16 = jnp.bfloat16
NX, NZ, NY, NC = 4, 8, 4, 2
LAST = (((1,), (1,)), ((), ()))
FIRST = (((0,), (0,)), ((), ()))


def dot(left, right, dims=None):
    if dims is None:
        return jnp.dot(left, right, preferred_element_type=F32)
    return lax.dot_general(left, right, dims, preferred_element_type=F32)


def rms(flat, gain):
    power = jnp.mean(flat * flat, axis=-1, keepdims=True)
    return flat * lax.rsqrt(power + eps) * gain


def gelu(h):
    cdf = 0.5 * (1.0 + jnp.tanh(0.7978845608028654 * (h + 0.044715 * (h * h * h))))
    return h * cdf


def div(n, d):
    return n // d if isinstance(n, int) else lax.div(n, jnp.int32(d))


def mod(n, d):
    return n % d if isinstance(n, int) else lax.rem(n, jnp.int32(d))


def place(x, z, y, core):
    return x * 2 + div(z, 4), mod(z, 4) * 8 + y * 2 + core


def kernel(
    stream_hbm, wv_hbm, wg_hbm, wo_hbm, within_hbm, across_hbm, ws_hbm, as_hbm,
    mix_hbm, final_hbm, up_hbm, down_hbm,
    result,
    stream, wv, wg, wo, within, across, ws, ascale, mix_gain, final_gain, up, down,
    wvt, wgt, wst, normed, gates,
    send1, recv1, send2, recv2, send3, recv3, flip1, flip2,
    in_sem, s1, r1, s2, r2, s3, r3,
):
    chan = lax.axis_index("chan")
    seq = lax.axis_index("seq")
    x, z = div(chan, 2), mod(chan, 2) * 4 + div(seq, 8)
    y, core = mod(div(seq, 2), 4), mod(seq, 2)
    zl, yc = div(seq, 8), mod(seq, 8)
    own = x * 8 + z

    def p_block(half, y_of, core_of):
        return 2 * mod(x + y_of + 2 * core_of + half, NX) + core_of

    def load(number, source, target):
        return pltpu.make_async_copy(source, target, in_sem.at[number])

    loads = [
        load(1, wv_hbm, wv), load(2, mix_hbm, mix_gain),
        load(3, wg_hbm, wg), load(4, within_hbm, within), load(5, ws_hbm, ws),
        load(6, across_hbm, across), load(7, as_hbm, ascale), load(8, wo_hbm, wo),
        load(9, final_hbm, final_gain), load(10, up_hbm, up), load(11, down_hbm, down),
    ]
    loads = dict(zip(range(1, 12), loads))
    for part in range(2):
        rows = pl.ds(8 * part, 8)
        loads[12 + part] = load(12 + part, stream_hbm.at[rows], stream.at[rows])
    for number in (1, 12, 13, 2, 3, 4, 5, 6, 7, 8, 9, 10, 11):
        loads[number].start()

    barrier = pltpu.get_barrier_semaphore()

    def greet(x_of, z_of, y_of, core_of):
        pl.semaphore_signal(
            barrier, inc=1, device_id=place(x_of, z_of, y_of, core_of), device_id_type=MESH
        )

    @pl.loop(1, NX * NZ)
    def _(i):
        greet(mod(x + div(i, NZ), NX), mod(z + mod(i, NZ), NZ), y, core)

    @pl.loop(1, NY * NC)
    def _(i):
        greet(x, z, mod(y + div(i, NC), NY), mod(core + mod(i, NC), NC))

    for half in range(2):
        @pl.loop(0, NX * NZ)
        def _(i):
            x_of = div(i, NZ)
            core_of = mod(chan, 2)
            greet(x_of, mod(i, NZ), mod(x - x_of - 2 * core_of - half + 2 * NX, NY), core_of)

    for number in (1, 2):
        loads[number].wait()
    wvt[...] = wv[...].astype(F32).T.reshape(32, 2, 8, 512).swapaxes(0, 1).reshape(2, 256, 512).astype(BF16)
    gain = mix_gain[...].astype(F32).reshape(1, 512)

    def values(half, pair, tokens):
        found = dot(wvt[half], tokens, LAST)
        split = [found[:, :128].reshape(32, 8, 128), found[:, 128:].reshape(32, 8, 128)]
        send1[half, :, pair] = jnp.concatenate(split, axis=1).astype(BF16)

    def send_values(half, first, count):
        rows = pl.ds(first, count)
        pltpu.make_async_copy(
            send1.at[half, own, rows], recv1.at[half, chan, zl, rows], r1.at[half]
        ).start()

        @pl.loop(1, NX * NZ)
        def _(i):
            x_of, z_of = mod(x + div(i, NZ), NX), mod(z + mod(i, NZ), NZ)
            pltpu.make_async_remote_copy(
                send1.at[half, x_of * 8 + z_of, rows], recv1.at[half, chan, zl, rows],
                s1.at[half], r1.at[half],
                device_id=place(x_of, z_of, y, core), device_id_type=MESH,
            ).start()

    for part in range(2):
        loads[12 + part].wait()

        @pl.loop(4 * part, 4 * part + 4)
        def _(pair):
            flat = stream[pl.ds(2 * pair, 2)].reshape(256, 512).astype(F32)
            tokens = rms(flat, gain).astype(BF16)
            normed[pair] = tokens
            values(0, pair, tokens)

        if part == 0:
            pl.semaphore_wait(barrier, NX * NZ - 1 + NY * NC - 1 + 2 * NX * NZ)
        send_values(0, 4 * part, 4)

    @pl.loop(0, 8)
    def _(pair):
        values(1, pair, normed[pair])

    send_values(1, 0, 8)

    loads[3].wait()
    wgt[...] = wg[...].astype(F32).T.astype(BF16)

    @pl.loop(0, 8)
    def _(pair):
        found = dot(wgt[...], normed[pair], LAST).astype(BF16)
        gates[2 * pair] = found[:, :128]
        gates[2 * pair + 1] = found[:, 128:]

    for number in range(4, 12):
        loads[number].wait()
    lower = lax.broadcasted_iota(jnp.int32, (256, 256), 0) >= lax.broadcasted_iota(jnp.int32, (256, 256), 1)
    for n in range(4):
        edge = pl.ds(256 * n, 256)
        within[edge, edge] = jnp.where(lower, within[edge, edge].astype(F32), 0.0).astype(BF16)
    for n in range(2):
        edge = pl.ds(256 * n, 256)
        across[edge, edge] = jnp.where(lower, across[edge, edge].astype(F32), 0.0).astype(BF16)
    picked = lax.broadcasted_iota(jnp.int32, (16, 64), 1) == 16 * zl + lax.broadcasted_iota(jnp.int32, (16, 64), 0)
    wst[...] = dot(picked.astype(F32).astype(BF16), ws[...])

    def middle_of(half):
        pltpu.make_async_copy(recv1.at[half], recv1.at[half], r1.at[half]).wait()
        for n in range(4):
            blocks = [recv1[half, k].reshape(512, 128) for k in range(2 * n + 2)]
            found = dot(
                jnp.concatenate(blocks, axis=1), within[pl.ds(256 * n, 256), pl.ds(0, 256 * (n + 1))], LAST
            )
            scale = wst[pl.ds(8 * half, 8), pl.ds(256 * n, 256)]
            scaled = (found.reshape(64, 8, 256) * scale[None]).reshape(512, 256)
            for side in range(2):
                flip1[side] = scaled[:, 128 * side : 128 * side + 128]
            for side in range(2):
                for c in range(8):
                    column = flip1[side, pl.ds(c, 64, stride=8), :]
                    send2[half, 2 * n + side, c] = column.astype(BF16).reshape(4, 16, 128)
        pltpu.make_async_copy(
            send2.at[half, p_block(half, y, core)], recv2.at[half, yc], r2.at[half]
        ).start()

        @pl.loop(1, NY * NC)
        def _(i):
            y_of, core_of = mod(y + div(i, NC), NY), mod(core + mod(i, NC), NC)
            pltpu.make_async_remote_copy(
                send2.at[half, p_block(half, y_of, core_of)], recv2.at[half, yc],
                s2.at[half], r2.at[half],
                device_id=place(x, z, y_of, core_of), device_id_type=MESH,
            ).start()

    def across_of(half):
        pltpu.make_async_copy(recv2.at[half], recv2.at[half], r2.at[half]).wait()
        for c in range(0, 8, 2):
            both = jnp.concatenate(
                [
                    jnp.concatenate([recv2[half, :, one, k].reshape(128, 128) for k in range(4)], axis=0)
                    for one in (c, c + 1)
                ],
                axis=1,
            )
            row = lax.broadcasted_iota(jnp.int32, (64, 256), 0)
            wanted = 16 * zl + 8 * half + c + lax.broadcasted_iota(jnp.int32, (64, 256), 1) // 128
            spread = (row == wanted).astype(F32).astype(BF16)
            for n in range(2):
                rows = pl.ds(256 * n, 256)
                found = dot(across[rows, pl.ds(0, 256 * (n + 1))], both[: 256 * (n + 1)])
                found = found * dot(ascale[:, rows], spread, FIRST)
                for side in range(2):
                    flip2[pl.ds(2048 * n + c + side, 256, stride=8), :] = found[:, 128 * side : 128 * side + 128]

        @pl.loop(0, 32)
        def _(block):
            start = pl.multiple_of(block * 128, 128)
            send3[half, block] = flip2[pl.ds(start, 128), :].reshape(8, 16, 128).astype(BF16)

    def send_mixed(half, first, count, sem):
        block = p_block(half, y, core)
        rows = pl.ds(first, count)

        def remote(i):
            zl_of, yc_of = mod(zl + mod(i, 4), 4), mod(yc + div(i, 4), 8)
            seq_of = zl_of * 8 + yc_of
            pltpu.make_async_remote_copy(
                send3.at[half, seq_of, rows], recv3.at[half, own, rows],
                s3.at[sem], r3.at[sem], device_id=(block, seq_of), device_id_type=MESH,
            ).start()

        @pl.when(block == chan)
        def _():
            pltpu.make_async_copy(
                send3.at[half, seq, rows], recv3.at[half, own, rows], r3.at[sem]
            ).start()

        @pl.when(block != chan)
        def _():
            remote(0)

        @pl.loop(1, 32)
        def _(i):
            remote(i)

    middle_of(0)
    across_of(0)
    send_mixed(0, 0, 8, 4)
    middle_of(1)
    across_of(1)
    for part in range(4):
        send_mixed(1, 2 * part, 2, part)

    pltpu.make_async_copy(recv3.at[0], recv3.at[0], r3.at[4]).wait()
    gain2 = final_gain[...].astype(F32).reshape(1, 512)
    for part in range(4):
        arrived = recv3.at[1, :, pl.ds(2 * part, 2)]
        pltpu.make_async_copy(arrived, arrived, r3.at[part]).wait()

        @pl.loop(2 * part, 2 * part + 2)
        def _(pair):
            halves = [recv3[half, :, pair].astype(F32) for half in range(2)]
            projected = []
            for one in range(2):
                mixed = jnp.concatenate([h[:, 8 * one : 8 * one + 8] for h in halves], axis=1)
                gated = mixed.reshape(512, 128) * gates[2 * pair + one].astype(F32)
                projected.append(dot(gated.astype(BF16), wo[...], FIRST))
            flat = stream[pl.ds(2 * pair, 2)].reshape(256, 512).astype(F32)
            middle = (flat + jnp.concatenate(projected, axis=0)).astype(BF16).astype(F32)
            renormed = rms(middle, gain2).astype(BF16)
            outer = []
            for k in range(4):
                inner = gelu(dot(renormed[:, 128 * k : 128 * k + 128], up[k])).astype(BF16)
                outer.append(dot(inner, down[k]))
            total = (middle + jnp.concatenate(outer, axis=1)).astype(BF16)
            result[pl.ds(2 * pair, 2)] = total.reshape(2, 128, 512)

    for half in range(2):
        sent = send1.at[half, pl.ds(0, 31)]
        pltpu.make_async_copy(sent, sent, s1.at[half]).wait()
        sent = send2.at[half, pl.ds(0, 7)]
        pltpu.make_async_copy(sent, sent, s2.at[half]).wait()
    for sem in range(5):
        rows = pl.ds(0, 8) if sem == 4 else pl.ds(2 * sem, 2)
        half = 0 if sem == 4 else 1
        rest = send3.at[half, pl.ds(1, 31), rows]
        pltpu.make_async_copy(rest, rest, s3.at[sem]).wait()

        @pl.when(p_block(half, y, core) != chan)
        def _():
            one = send3.at[half, 0, rows]
            pltpu.make_async_copy(one, one, s3.at[sem]).wait()


def body(
    stream, weight_value, weight_gate, weight_out, within_factor, across_factor,
    within_scale, across_scale, mix_gain, final_gain, block_up, block_down,
):
    args = (
        stream, weight_value, weight_gate, weight_out, within_factor, across_factor,
        within_scale.T, across_scale.T, mix_gain, final_gain,
        block_up, block_down,
    )
    anywhere = pl.BlockSpec(memory_space=pl.ANY)
    return pl.pallas_call(
        kernel,
        out_shape=pltpu.VMEM(stream.shape, BF16),
        in_specs=[anywhere] * len(args),
        out_specs=pl.BlockSpec(memory_space=pltpu.VMEM),
        scratch_shapes=[pltpu.VMEM(a.shape, BF16) for a in args] + [
            pltpu.VMEM((2, 256, 512), BF16),
            pltpu.VMEM((512, 512), BF16),
            pltpu.VMEM((16, 1024), F32),
            pltpu.VMEM((8, 256, 512), BF16),
            pltpu.VMEM((16, 512, 128), BF16),
            pltpu.VMEM((2, 32, 8, 16, 128), BF16),
            pltpu.VMEM((2, 8, 4, 8, 16, 128), BF16),
            pltpu.VMEM((2, 8, 8, 4, 16, 128), BF16),
            pltpu.VMEM((2, 8, 8, 4, 16, 128), BF16),
            pltpu.VMEM((2, 32, 8, 16, 128), BF16),
            pltpu.VMEM((2, 32, 8, 16, 128), BF16),
            pltpu.VMEM((2, 512, 128), F32),
            pltpu.VMEM((4096, 128), F32),
            pltpu.SemaphoreType.DMA((14,)),
            pltpu.SemaphoreType.DMA((2,)),
            pltpu.SemaphoreType.DMA((2,)),
            pltpu.SemaphoreType.DMA((2,)),
            pltpu.SemaphoreType.DMA((2,)),
            pltpu.SemaphoreType.DMA((5,)),
            pltpu.SemaphoreType.DMA((5,)),
        ],
        compiler_params=pltpu.CompilerParams(
            collective_id=0, has_side_effects=True, vmem_limit_bytes=56 * 2**20
        ),
        cost_estimate=pl.CostEstimate(
            flops=9 * 10**9, bytes_accessed=12 * 2**20, transcendentals=2**22
        ),
        name="mixer",
    )(*args)


def solution(mesh):
    placed = (
        P("seq", "chan", None), P(), P(), P(), P(), P(), P(None, "chan"), P(None, "chan"),
        P(), P(), P(), P(),
    )
    return jax.shard_map(
        body, mesh=mesh, in_specs=placed, out_specs=P("seq", "chan", None), check_vma=False
    )
```

```python
import jax
import jax.numpy as jnp
from jax import lax
from jax.experimental import pallas as pl
from jax.experimental.pallas import tpu as pltpu
from jax.sharding import PartitionSpec as P

eps = 1e-05
MESH = pl.DeviceIdType.MESH
F32 = jnp.float32
BF16 = jnp.bfloat16
GT = jnp.bfloat16
PARTS = 4
PP = 8 // PARTS
NX, NZ, NY, NC = 4, 8, 4, 2
LAST = (((1,), (1,)), ((), ()))
FIRST = (((0,), (0,)), ((), ()))


def dot(left, right, dims=None):
    if dims is None:
        return jnp.dot(left, right, preferred_element_type=F32)
    return lax.dot_general(left, right, dims, preferred_element_type=F32)


def rms(flat, gain):
    power = jnp.mean(flat * flat, axis=-1, keepdims=True)
    return flat * lax.rsqrt(power + eps) * gain


def gelu(h):
    bent = jnp.tanh(h * (0.7978845608028654 + 0.035677408136300125 * (h * h)))
    half = 0.5 * h
    return half + half * bent


def halves_first(weight, axis_rows):
    grouped = weight.reshape(32, 2, 8, axis_rows).swapaxes(0, 1)
    return grouped.reshape(2, 256, axis_rows).astype(BF16)


def div(n, d):
    return n // d if isinstance(n, int) else lax.div(n, jnp.int32(d))


def mod(n, d):
    return n % d if isinstance(n, int) else lax.rem(n, jnp.int32(d))


def place(x, z, y, core):
    return x * 2 + div(z, 4), mod(z, 4) * 8 + y * 2 + core


def kernel(
    stream_hbm, wv_hbm, wg_hbm, wo_hbm, within_hbm, across_hbm, ws_hbm, as_hbm,
    mix_hbm, final_hbm, up_hbm, down_hbm,
    result,
    stream, wv, wg, wo, within, across, ws, ascale, mix_gain, final_gain, up, down,
    wvt, wgt, wot, partial, wst, normed, gates,
    send1, recv1, send2, recv2, send3, recv3, flip1, flip2,
    in_sem, s1, r1, s2, r2, s3, r3,
):
    chan = lax.axis_index("chan")
    seq = lax.axis_index("seq")
    x, z = div(chan, 2), mod(chan, 2) * 4 + div(seq, 8)
    y, core = mod(div(seq, 2), 4), mod(seq, 2)
    zl, yc = div(seq, 8), mod(seq, 8)
    own = x * 8 + z

    def p_block(half, y_of, core_of):
        return 2 * mod(x + y_of + 2 * core_of + half, NX) + core_of

    def load(number, source, target):
        return pltpu.make_async_copy(source, target, in_sem.at[number])

    loads = [
        load(1, wv_hbm, wv), load(2, mix_hbm, mix_gain),
        load(3, wg_hbm, wg), load(4, within_hbm, within), load(5, ws_hbm, ws),
        load(6, across_hbm, across), load(7, as_hbm, ascale), load(8, wo_hbm, wo),
        load(9, final_hbm, final_gain), load(10, up_hbm, up), load(11, down_hbm, down),
    ]
    loads = dict(zip(range(1, 12), loads))
    for part in range(2):
        rows = pl.ds(8 * part, 8)
        loads[12 + part] = load(12 + part, stream_hbm.at[rows], stream.at[rows])
    for number in (1, 12, 13, 2, 3, 4, 5, 6, 7, 8, 9, 10, 11):
        loads[number].start()

    barrier = pltpu.get_barrier_semaphore()

    def greet(x_of, z_of, y_of, core_of):
        pl.semaphore_signal(
            barrier, inc=1, device_id=place(x_of, z_of, y_of, core_of), device_id_type=MESH
        )

    @pl.loop(1, NX * NZ)
    def _(i):
        greet(mod(x + div(i, NZ), NX), mod(z + mod(i, NZ), NZ), y, core)

    @pl.loop(1, NY * NC)
    def _(i):
        greet(x, z, mod(y + div(i, NC), NY), mod(core + mod(i, NC), NC))

    for half in range(2):
        @pl.loop(0, NX * NZ)
        def _(i):
            x_of = div(i, NZ)
            core_of = mod(chan, 2)
            greet(x_of, mod(i, NZ), mod(x - x_of - 2 * core_of - half + 2 * NX, NY), core_of)

    for number in (1, 2):
        loads[number].wait()
    wvt[...] = halves_first(wv[...].astype(F32).T, 512)
    gain = mix_gain[...].astype(F32).reshape(1, 512)

    def values(half, pair, tokens):
        found = dot(wvt[half], tokens, LAST)
        split = [found[:, :128].reshape(32, 8, 128), found[:, 128:].reshape(32, 8, 128)]
        send1[half, :, pair] = jnp.concatenate(split, axis=1).astype(BF16)

    def send_values(half, first, count):
        rows = pl.ds(first, count)
        pltpu.make_async_copy(
            send1.at[half, own, rows], recv1.at[half, chan, zl, rows], r1.at[half]
        ).start()

        @pl.loop(1, NX * NZ)
        def _(i):
            x_of, z_of = mod(x + div(i, NZ), NX), mod(z + mod(i, NZ), NZ)
            pltpu.make_async_remote_copy(
                send1.at[half, x_of * 8 + z_of, rows], recv1.at[half, chan, zl, rows],
                s1.at[half], r1.at[half],
                device_id=place(x_of, z_of, y, core), device_id_type=MESH,
            ).start()

    for part in range(2):
        loads[12 + part].wait()

        @pl.loop(4 * part, 4 * part + 4)
        def _(pair):
            flat = stream[pl.ds(2 * pair, 2)].reshape(256, 512).astype(F32)
            tokens = rms(flat, gain).astype(BF16)
            normed[pair] = tokens
            values(0, pair, tokens)

        if part == 0:
            pl.semaphore_wait(barrier, NX * NZ - 1 + NY * NC - 1 + 2 * NX * NZ)
        send_values(0, 4 * part, 4)

    @pl.loop(0, 8)
    def _(pair):
        values(1, pair, normed[pair])

    send_values(1, 0, 8)

    loads[3].wait()
    wgt[...] = halves_first(wg[...].astype(F32).T, 512)

    @pl.loop(0, 8)
    def _(pair):
        for half in range(2):
            found = dot(wgt[half], normed[pair], LAST).astype(BF16)
            gates[half, 2 * pair] = found[:, :128]
            gates[half, 2 * pair + 1] = found[:, 128:]

    loads[8].wait()
    wot[...] = halves_first(wo[...].astype(F32), 512)

    for number in (4, 5, 6, 7, 9, 10, 11):
        loads[number].wait()
    lower = lax.broadcasted_iota(jnp.int32, (256, 256), 0) >= lax.broadcasted_iota(jnp.int32, (256, 256), 1)
    for n in range(4):
        edge = pl.ds(256 * n, 256)
        within[edge, edge] = jnp.where(lower, within[edge, edge].astype(F32), 0.0).astype(BF16)
    for n in range(2):
        edge = pl.ds(256 * n, 256)
        across[edge, edge] = jnp.where(lower, across[edge, edge].astype(F32), 0.0).astype(BF16)
    picked = lax.broadcasted_iota(jnp.int32, (16, 64), 1) == 16 * zl + lax.broadcasted_iota(jnp.int32, (16, 64), 0)
    wst[...] = dot(picked.astype(F32).astype(BF16), ws[...])

    def middle_of(half):
        pltpu.make_async_copy(recv1.at[half], recv1.at[half], r1.at[half]).wait()
        for n in range(4):
            blocks = [recv1[half, k].reshape(512, 128) for k in range(2 * n + 2)]
            found = dot(
                jnp.concatenate(blocks, axis=1), within[pl.ds(256 * n, 256), pl.ds(0, 256 * (n + 1))], LAST
            )
            scale = wst[pl.ds(8 * half, 8), pl.ds(256 * n, 256)]
            scaled = (found.reshape(64, 8, 256) * scale[None]).reshape(512, 256)
            for side in range(2):
                flip1[side] = scaled[:, 128 * side : 128 * side + 128]
            for side in range(2):
                for c in range(8):
                    column = flip1[side, pl.ds(c, 64, stride=8), :]
                    send2[half, 2 * n + side, c] = column.astype(BF16).reshape(4, 16, 128)
        pltpu.make_async_copy(
            send2.at[half, p_block(half, y, core)], recv2.at[half, yc], r2.at[half]
        ).start()

        @pl.loop(1, NY * NC)
        def _(i):
            y_of, core_of = mod(y + div(i, NC), NY), mod(core + mod(i, NC), NC)
            pltpu.make_async_remote_copy(
                send2.at[half, p_block(half, y_of, core_of)], recv2.at[half, yc],
                s2.at[half], r2.at[half],
                device_id=place(x, z, y_of, core_of), device_id_type=MESH,
            ).start()

    def across_of(half):
        pltpu.make_async_copy(recv2.at[half], recv2.at[half], r2.at[half]).wait()
        for c in range(0, 8, 2):
            both = jnp.concatenate(
                [
                    jnp.concatenate([recv2[half, :, one, k].reshape(128, 128) for k in range(4)], axis=0)
                    for one in (c, c + 1)
                ],
                axis=1,
            )
            row = lax.broadcasted_iota(jnp.int32, (64, 256), 0)
            wanted = 16 * zl + 8 * half + c + lax.broadcasted_iota(jnp.int32, (64, 256), 1) // 128
            spread = (row == wanted).astype(F32).astype(BF16)
            for n in range(2):
                rows = pl.ds(256 * n, 256)
                found = dot(across[rows, pl.ds(0, 256 * (n + 1))], both[: 256 * (n + 1)])
                found = found * dot(ascale[:, rows], spread, FIRST)
                for side in range(2):
                    flip2[pl.ds(2048 * n + c + side, 256, stride=8), :] = found[:, 128 * side : 128 * side + 128]

        @pl.loop(0, 32)
        def _(block):
            start = pl.multiple_of(block * 128, 128)
            send3[half, block] = flip2[pl.ds(start, 128), :].reshape(8, 16, 128).astype(BF16)

    def send_mixed(half, first, count, sem):
        block = p_block(half, y, core)
        rows = pl.ds(first, count)

        def remote(i):
            zl_of, yc_of = mod(zl + mod(i, 4), 4), mod(yc + div(i, 4), 8)
            seq_of = zl_of * 8 + yc_of
            pltpu.make_async_remote_copy(
                send3.at[half, seq_of, rows], recv3.at[half, own, rows],
                s3.at[sem], r3.at[sem], device_id=(block, seq_of), device_id_type=MESH,
            ).start()

        @pl.when(block == chan)
        def _():
            pltpu.make_async_copy(
                send3.at[half, seq, rows], recv3.at[half, own, rows], r3.at[sem]
            ).start()

        @pl.when(block != chan)
        def _():
            remote(0)

        @pl.loop(1, 32)
        def _(i):
            remote(i)

    middle_of(0)
    across_of(0)
    send_mixed(0, 0, 8, PARTS)
    middle_of(1)
    across_of(1)
    for part in range(PARTS):
        send_mixed(1, PP * part, PP, part)

    pltpu.make_async_copy(recv3.at[0], recv3.at[0], r3.at[PARTS]).wait()

    def projected(half, pair):
        mixed = recv3[half, :, pair].astype(F32)
        gated = [
            (mixed[:, 8 * one : 8 * one + 8].reshape(256, 128) * gates[half, 2 * pair + one].astype(F32)).astype(BF16)
            for one in range(2)
        ]
        return dot(jnp.concatenate(gated, axis=1), wot[half], FIRST)

    @pl.loop(0, 8)
    def _(pair):
        flat = stream[pl.ds(2 * pair, 2)].reshape(256, 512).astype(F32)
        partial[pair] = flat + projected(0, pair)

    gain2 = final_gain[...].astype(F32).reshape(1, 512)
    for part in range(PARTS):
        arrived = recv3.at[1, :, pl.ds(PP * part, PP)]
        pltpu.make_async_copy(arrived, arrived, r3.at[part]).wait()
        pairs = range(PP * part, PP * part + PP)
        middle = jnp.concatenate([partial[pair] + projected(1, pair) for pair in pairs], axis=0)
        middle = middle.astype(BF16).astype(F32)
        renormed = rms(middle, gain2).astype(BF16)
        outer = []
        for k in range(4):
            inner = gelu(dot(renormed[:, 128 * k : 128 * k + 128], up[k]).astype(GT)).astype(BF16)
            outer.append(dot(inner, down[k]))
        total = (middle + jnp.concatenate(outer, axis=1)).astype(BF16)
        result[pl.ds(2 * PP * part, 2 * PP)] = total.reshape(2 * PP, 128, 512)

    for half in range(2):
        sent = send1.at[half, pl.ds(0, 31)]
        pltpu.make_async_copy(sent, sent, s1.at[half]).wait()
        sent = send2.at[half, pl.ds(0, 7)]
        pltpu.make_async_copy(sent, sent, s2.at[half]).wait()
    for sem in range(PARTS + 1):
        rows = pl.ds(0, 8) if sem == PARTS else pl.ds(PP * sem, PP)
        half = 0 if sem == PARTS else 1
        rest = send3.at[half, pl.ds(1, 31), rows]
        pltpu.make_async_copy(rest, rest, s3.at[sem]).wait()

        @pl.when(p_block(half, y, core) != chan)
        def _():
            one = send3.at[half, 0, rows]
            pltpu.make_async_copy(one, one, s3.at[sem]).wait()


def body(
    stream, weight_value, weight_gate, weight_out, within_factor, across_factor,
    within_scale, across_scale, mix_gain, final_gain, block_up, block_down,
):
    args = (
        stream, weight_value, weight_gate, weight_out, within_factor, across_factor,
        within_scale.T, across_scale.T, mix_gain, final_gain,
        block_up, block_down,
    )
    anywhere = pl.BlockSpec(memory_space=pl.ANY)
    return pl.pallas_call(
        kernel,
        out_shape=pltpu.VMEM(stream.shape, BF16),
        in_specs=[anywhere] * len(args),
        out_specs=pl.BlockSpec(memory_space=pltpu.VMEM),
        scratch_shapes=[pltpu.VMEM(a.shape, BF16) for a in args] + [
            pltpu.VMEM((2, 256, 512), BF16),
            pltpu.VMEM((2, 256, 512), BF16),
            pltpu.VMEM((2, 256, 512), BF16),
            pltpu.VMEM((8, 256, 512), F32),
            pltpu.VMEM((16, 1024), F32),
            pltpu.VMEM((8, 256, 512), BF16),
            pltpu.VMEM((2, 16, 256, 128), BF16),
            pltpu.VMEM((2, 32, 8, 16, 128), BF16),
            pltpu.VMEM((2, 8, 4, 8, 16, 128), BF16),
            pltpu.VMEM((2, 8, 8, 4, 16, 128), BF16),
            pltpu.VMEM((2, 8, 8, 4, 16, 128), BF16),
            pltpu.VMEM((2, 32, 8, 16, 128), BF16),
            pltpu.VMEM((2, 32, 8, 16, 128), BF16),
            pltpu.VMEM((2, 512, 128), F32),
            pltpu.VMEM((4096, 128), F32),
            pltpu.SemaphoreType.DMA((14,)),
            pltpu.SemaphoreType.DMA((2,)),
            pltpu.SemaphoreType.DMA((2,)),
            pltpu.SemaphoreType.DMA((2,)),
            pltpu.SemaphoreType.DMA((2,)),
            pltpu.SemaphoreType.DMA((PARTS + 1,)),
            pltpu.SemaphoreType.DMA((PARTS + 1,)),
        ],
        compiler_params=pltpu.CompilerParams(
            collective_id=0, has_side_effects=True, vmem_limit_bytes=56 * 2**20
        ),
        cost_estimate=pl.CostEstimate(
            flops=9 * 10**9, bytes_accessed=12 * 2**20, transcendentals=2**22
        ),
        name="mixer",
    )(*args)


def solution(mesh):
    placed = (
        P("seq", "chan", None), P(), P(), P(), P(), P(), P(None, "chan"), P(None, "chan"),
        P(), P(), P(), P(),
    )
    return jax.shard_map(
        body, mesh=mesh, in_specs=placed, out_specs=P("seq", "chan", None), check_vma=False
    )
```

```python
import jax
import jax.numpy as jnp
from jax import lax
from jax.experimental import pallas as pl
from jax.experimental.pallas import tpu as pltpu
from jax.sharding import PartitionSpec as P

eps = 1e-05
MESH = pl.DeviceIdType.MESH
F32 = jnp.float32
BF16 = jnp.bfloat16
GT = jnp.bfloat16
MAPH = 0
PARTS = 4
PP = 8 // PARTS
NX, NZ, NY, NC = 4, 8, 4, 2
LAST = (((1,), (1,)), ((), ()))
FIRST = (((0,), (0,)), ((), ()))


def dot(left, right, dims=None):
    if dims is None:
        return jnp.dot(left, right, preferred_element_type=F32)
    return lax.dot_general(left, right, dims, preferred_element_type=F32)


def rms(flat, gain):
    power = jnp.mean(flat * flat, axis=-1, keepdims=True)
    return flat * lax.rsqrt(power + eps) * gain


def gelu(h):
    bent = jnp.tanh(h * (0.7978845608028654 + 0.035677408136300125 * (h * h)))
    half = 0.5 * h
    return half + half * bent


def halves_first(weight, axis_rows):
    grouped = weight.reshape(32, 2, 8, axis_rows).swapaxes(0, 1)
    return grouped.reshape(2, 256, axis_rows).astype(BF16)


def div(n, d):
    return n // d if isinstance(n, int) else lax.div(n, jnp.int32(d))


def mod(n, d):
    return n % d if isinstance(n, int) else lax.rem(n, jnp.int32(d))


def place(x, z, y, core):
    return x * 2 + div(z, 4), mod(z, 4) * 8 + y * 2 + core


def kernel(
    stream_hbm, wv_hbm, wg_hbm, wo_hbm, within_hbm, across_hbm, ws_hbm, as_hbm,
    mix_hbm, final_hbm, up_hbm, down_hbm,
    result,
    stream, wv, wg, wo, within, across, ws, ascale, mix_gain, final_gain, up, down,
    wvt, wgt, wot, partial, wst, normed, gates,
    send1, recv1, send2, recv2, send3, recv3, flip1, flip2,
    in_sem, s1, r1, s2, r2, s3, r3,
):
    chan = lax.axis_index("chan")
    seq = lax.axis_index("seq")
    x, z = div(chan, 2), mod(chan, 2) * 4 + div(seq, 8)
    y, core = mod(div(seq, 2), 4), mod(seq, 2)
    zl, yc = div(seq, 8), mod(seq, 8)
    own = x * 8 + z

    def p_block(half, y_of, core_of):
        return 2 * mod(x + y_of + 2 * core_of + half, NX) + mod(core_of + MAPH * half, NC)

    def load(number, source, target):
        return pltpu.make_async_copy(source, target, in_sem.at[number])

    loads = [
        load(1, wv_hbm, wv), load(2, mix_hbm, mix_gain),
        load(3, wg_hbm, wg), load(4, within_hbm, within), load(5, ws_hbm, ws),
        load(6, across_hbm, across), load(7, as_hbm, ascale), load(8, wo_hbm, wo),
        load(9, final_hbm, final_gain), load(10, up_hbm, up), load(11, down_hbm, down),
    ]
    loads = dict(zip(range(1, 12), loads))
    for part in range(2):
        rows = pl.ds(8 * part, 8)
        loads[12 + part] = load(12 + part, stream_hbm.at[rows], stream.at[rows])
    for number in (1, 12, 13, 2, 3, 4, 5, 6, 7, 8, 9, 10, 11):
        loads[number].start()

    barrier = pltpu.get_barrier_semaphore()

    def greet(x_of, z_of, y_of, core_of):
        pl.semaphore_signal(
            barrier, inc=1, device_id=place(x_of, z_of, y_of, core_of), device_id_type=MESH
        )

    @pl.loop(1, NX * NZ)
    def _(i):
        greet(mod(x + div(i, NZ), NX), mod(z + mod(i, NZ), NZ), y, core)

    @pl.loop(1, NY * NC)
    def _(i):
        greet(x, z, mod(y + div(i, NC), NY), mod(core + mod(i, NC), NC))

    for half in range(2):
        @pl.loop(0, NX * NZ)
        def _(i):
            x_of = div(i, NZ)
            core_of = mod(chan + MAPH * half, NC)
            greet(x_of, mod(i, NZ), mod(x - x_of - 2 * core_of - half + 2 * NX, NY), core_of)

    for number in (1, 2):
        loads[number].wait()
    wvt[...] = halves_first(wv[...].astype(F32).T, 512)
    gain = mix_gain[...].astype(F32).reshape(1, 512)

    def values(half, pair, tokens):
        found = dot(wvt[half], tokens, LAST)
        split = [found[:, :128].reshape(32, 8, 128), found[:, 128:].reshape(32, 8, 128)]
        send1[half, :, pair] = jnp.concatenate(split, axis=1).astype(BF16)

    def send_values(half, block):
        rows = pl.ds(4 * block, 4)
        pltpu.make_async_copy(
            send1.at[half, own, rows], recv1.at[half, block, chan, zl], r1.at[half, block]
        ).start()

        @pl.loop(1, NX * NZ)
        def _(i):
            x_of, z_of = mod(x + div(i, NZ), NX), mod(z + mod(i, NZ), NZ)
            pltpu.make_async_remote_copy(
                send1.at[half, x_of * 8 + z_of, rows], recv1.at[half, block, chan, zl],
                s1.at[half], r1.at[half, block],
                device_id=place(x_of, z_of, y, core), device_id_type=MESH,
            ).start()

    for block in range(2):
        loads[12 + block].wait()

        @pl.loop(4 * block, 4 * block + 4)
        def _(pair):
            flat = stream[pl.ds(2 * pair, 2)].reshape(256, 512).astype(F32)
            tokens = rms(flat, gain).astype(BF16)
            normed[pair] = tokens
            values(0, pair, tokens)

        if block == 0:
            pl.semaphore_wait(barrier, NX * NZ - 1 + NY * NC - 1 + 2 * NX * NZ)
        send_values(0, block)

    for block in range(2):
        @pl.loop(4 * block, 4 * block + 4)
        def _(pair):
            values(1, pair, normed[pair])

        send_values(1, block)

    loads[3].wait()
    wgt[...] = halves_first(wg[...].astype(F32).T, 512)

    @pl.loop(0, 8)
    def _(pair):
        for half in range(2):
            found = dot(wgt[half], normed[pair], LAST).astype(BF16)
            gates[half, 2 * pair] = found[:, :128]
            gates[half, 2 * pair + 1] = found[:, 128:]

    loads[8].wait()
    wot[...] = halves_first(wo[...].astype(F32), 512)

    for number in (4, 5, 6, 7, 9, 10, 11):
        loads[number].wait()
    lower = lax.broadcasted_iota(jnp.int32, (256, 256), 0) >= lax.broadcasted_iota(jnp.int32, (256, 256), 1)
    for n in range(4):
        edge = pl.ds(256 * n, 256)
        within[edge, edge] = jnp.where(lower, within[edge, edge].astype(F32), 0.0).astype(BF16)
    for n in range(2):
        edge = pl.ds(256 * n, 256)
        across[edge, edge] = jnp.where(lower, across[edge, edge].astype(F32), 0.0).astype(BF16)
    old = lax.broadcasted_iota(jnp.int32, (256, 256), 0)
    new = lax.broadcasted_iota(jnp.int32, (256, 256), 1)
    moved = (old & 119) + ((old >> 3) & 1) * 128 + (old >> 7) * 8
    swap = (moved == new).astype(F32).astype(BF16)
    for n in range(2):
        edge = pl.ds(256 * n, 256)
        across[:, edge] = dot(across[:, edge], swap).astype(BF16)
    picked = lax.broadcasted_iota(jnp.int32, (16, 64), 1) == 16 * zl + lax.broadcasted_iota(jnp.int32, (16, 64), 0)
    wst[...] = dot(picked.astype(F32).astype(BF16), ws[...])

    def middle_of(half, block):
        arrived = recv1.at[half, block]
        pltpu.make_async_copy(arrived, arrived, r1.at[half, block]).wait()
        for n in range(4):
            blocks = [recv1[half, block, k].reshape(256, 128) for k in range(2 * n + 2)]
            found = dot(
                jnp.concatenate(blocks, axis=1), within[pl.ds(256 * n, 256), pl.ds(0, 256 * (n + 1))], LAST
            )
            scale = wst[pl.ds(8 * half, 8), pl.ds(256 * n, 256)]
            scaled = (found.reshape(32, 8, 256) * scale[None]).reshape(256, 256)
            for side in range(2):
                flip1[n, side] = scaled[:, 128 * side : 128 * side + 128]
            for side in range(2):
                for c in range(8):
                    column = flip1[n, side, pl.ds(c, 32, stride=8), :]
                    send2[half, block, 2 * n + side, c] = column.astype(BF16).reshape(2, 16, 128)
        pltpu.make_async_copy(
            send2.at[half, block, p_block(half, y, core)], recv2.at[half, block, yc], r2.at[half]
        ).start()

        @pl.loop(1, NY * NC)
        def _(i):
            y_of, core_of = mod(y + div(i, NC), NY), mod(core + mod(i, NC), NC)
            pltpu.make_async_remote_copy(
                send2.at[half, block, p_block(half, y_of, core_of)], recv2.at[half, block, yc],
                s2.at[half], r2.at[half],
                device_id=place(x, z, y_of, core_of), device_id_type=MESH,
            ).start()

    def across_of(half):
        pltpu.make_async_copy(recv2.at[half], recv2.at[half], r2.at[half]).wait()
        for c in range(0, 8, 2):
            both = jnp.concatenate(
                [
                    jnp.concatenate([
                            recv2[half, block, :, one, k].reshape(128, 128)
                            for k in range(2)
                            for block in range(2)
                        ], axis=0)
                    for one in (c, c + 1)
                ],
                axis=1,
            )
            row = lax.broadcasted_iota(jnp.int32, (64, 256), 0)
            wanted = 16 * zl + 8 * half + c + lax.broadcasted_iota(jnp.int32, (64, 256), 1) // 128
            spread = (row == wanted).astype(F32).astype(BF16)
            for n in range(2):
                rows = pl.ds(256 * n, 256)
                found = dot(across[rows, pl.ds(0, 256 * (n + 1))], both[: 256 * (n + 1)])
                found = found * dot(ascale[:, rows], spread, FIRST)
                for side in range(2):
                    flip2[pl.ds(2048 * n + c + side, 256, stride=8), :] = found[:, 128 * side : 128 * side + 128]

        @pl.loop(0, 32)
        def _(block):
            start = pl.multiple_of(block * 128, 128)
            send3[half, block] = flip2[pl.ds(start, 128), :].reshape(8, 16, 128).astype(BF16)

    def send_mixed(half, first, count, sem):
        block = p_block(half, y, core)
        rows = pl.ds(first, count)

        def remote(i):
            zl_of, yc_of = mod(zl + mod(i, 4), 4), mod(yc + div(i, 4), 8)
            seq_of = zl_of * 8 + yc_of
            pltpu.make_async_remote_copy(
                send3.at[half, seq_of, rows], recv3.at[half, own, rows],
                s3.at[sem], r3.at[sem], device_id=(block, seq_of), device_id_type=MESH,
            ).start()

        @pl.when(block == chan)
        def _():
            pltpu.make_async_copy(
                send3.at[half, seq, rows], recv3.at[half, own, rows], r3.at[sem]
            ).start()

        @pl.when(block != chan)
        def _():
            remote(0)

        @pl.loop(1, 32)
        def _(i):
            remote(i)

    middle_of(0, 0)
    middle_of(0, 1)
    across_of(0)
    send_mixed(0, 0, 8, PARTS)
    middle_of(1, 0)
    middle_of(1, 1)
    across_of(1)
    for part in range(PARTS):
        send_mixed(1, PP * part, PP, part)

    pltpu.make_async_copy(recv3.at[0], recv3.at[0], r3.at[PARTS]).wait()

    def projected(half, pair):
        mixed = recv3[half, :, pair].astype(F32)
        gated = [
            (mixed[:, 8 * one : 8 * one + 8].reshape(256, 128) * gates[half, 2 * pair + one].astype(F32)).astype(BF16)
            for one in range(2)
        ]
        return dot(jnp.concatenate(gated, axis=1), wot[half], FIRST)

    @pl.loop(0, 8)
    def _(pair):
        flat = stream[pl.ds(2 * pair, 2)].reshape(256, 512).astype(F32)
        partial[pair] = flat + projected(0, pair)

    gain2 = final_gain[...].astype(F32).reshape(1, 512)
    for part in range(PARTS):
        arrived = recv3.at[1, :, pl.ds(PP * part, PP)]
        pltpu.make_async_copy(arrived, arrived, r3.at[part]).wait()
        pairs = range(PP * part, PP * part + PP)
        middle = jnp.concatenate([partial[pair] + projected(1, pair) for pair in pairs], axis=0)
        middle = middle.astype(BF16).astype(F32)
        renormed = rms(middle, gain2).astype(BF16)
        outer = []
        for k in range(4):
            inner = gelu(dot(renormed[:, 128 * k : 128 * k + 128], up[k]).astype(GT)).astype(BF16)
            outer.append(dot(inner, down[k]))
        total = (middle + jnp.concatenate(outer, axis=1)).astype(BF16)
        result[pl.ds(2 * PP * part, 2 * PP)] = total.reshape(2 * PP, 128, 512)

    for half in range(2):
        sent = send1.at[half, pl.ds(0, 31)]
        pltpu.make_async_copy(sent, sent, s1.at[half]).wait()
        sent = send2.at[half, :, pl.ds(0, 7)]
        pltpu.make_async_copy(sent, sent, s2.at[half]).wait()
    for sem in range(PARTS + 1):
        rows = pl.ds(0, 8) if sem == PARTS else pl.ds(PP * sem, PP)
        half = 0 if sem == PARTS else 1
        rest = send3.at[half, pl.ds(1, 31), rows]
        pltpu.make_async_copy(rest, rest, s3.at[sem]).wait()

        @pl.when(p_block(half, y, core) != chan)
        def _():
            one = send3.at[half, 0, rows]
            pltpu.make_async_copy(one, one, s3.at[sem]).wait()


def body(
    stream, weight_value, weight_gate, weight_out, within_factor, across_factor,
    within_scale, across_scale, mix_gain, final_gain, block_up, block_down,
):
    args = (
        stream, weight_value, weight_gate, weight_out, within_factor, across_factor,
        within_scale.T, across_scale.T, mix_gain, final_gain,
        block_up, block_down,
    )
    anywhere = pl.BlockSpec(memory_space=pl.ANY)
    return pl.pallas_call(
        kernel,
        out_shape=pltpu.VMEM(stream.shape, BF16),
        in_specs=[anywhere] * len(args),
        out_specs=pl.BlockSpec(memory_space=pltpu.VMEM),
        scratch_shapes=[pltpu.VMEM(a.shape, BF16) for a in args] + [
            pltpu.VMEM((2, 256, 512), BF16),
            pltpu.VMEM((2, 256, 512), BF16),
            pltpu.VMEM((2, 256, 512), BF16),
            pltpu.VMEM((8, 256, 512), F32),
            pltpu.VMEM((16, 1024), F32),
            pltpu.VMEM((8, 256, 512), BF16),
            pltpu.VMEM((2, 16, 256, 128), BF16),
            pltpu.VMEM((2, 32, 8, 16, 128), BF16),
            pltpu.VMEM((2, 2, 8, 4, 4, 16, 128), BF16),
            pltpu.VMEM((2, 2, 8, 8, 2, 16, 128), BF16),
            pltpu.VMEM((2, 2, 8, 8, 2, 16, 128), BF16),
            pltpu.VMEM((2, 32, 8, 16, 128), BF16),
            pltpu.VMEM((2, 32, 8, 16, 128), BF16),
            pltpu.VMEM((4, 2, 256, 128), F32),
            pltpu.VMEM((4096, 128), F32),
            pltpu.SemaphoreType.DMA((14,)),
            pltpu.SemaphoreType.DMA((2,)),
            pltpu.SemaphoreType.DMA((2, 2)),
            pltpu.SemaphoreType.DMA((2,)),
            pltpu.SemaphoreType.DMA((2,)),
            pltpu.SemaphoreType.DMA((PARTS + 1,)),
            pltpu.SemaphoreType.DMA((PARTS + 1,)),
        ],
        compiler_params=pltpu.CompilerParams(
            collective_id=0, has_side_effects=True, vmem_limit_bytes=56 * 2**20
        ),
        cost_estimate=pl.CostEstimate(
            flops=9 * 10**9, bytes_accessed=12 * 2**20, transcendentals=2**22
        ),
        name="mixer",
    )(*args)


def solution(mesh):
    placed = (
        P("seq", "chan", None), P(), P(), P(), P(), P(), P(None, "chan"), P(None, "chan"),
        P(), P(), P(), P(),
    )
    return jax.shard_map(
        body, mesh=mesh, in_specs=placed, out_specs=P("seq", "chan", None), check_vma=False
    )
```

```python
import jax
import jax.numpy as jnp
from jax import lax
from jax.experimental import pallas as pl
from jax.experimental.pallas import tpu as pltpu
from jax.sharding import PartitionSpec as P

eps = 1e-05
MESH = pl.DeviceIdType.MESH
F32 = jnp.float32
BF16 = jnp.bfloat16
GT = jnp.bfloat16
PARTS = 4
PP = 8 // PARTS
NX, NZ, NY, NC = 4, 8, 4, 2
LAST = (((1,), (1,)), ((), ()))
FIRST = (((0,), (0,)), ((), ()))


def dot(left, right, dims=None):
    if dims is None:
        return jnp.dot(left, right, preferred_element_type=F32)
    return lax.dot_general(left, right, dims, preferred_element_type=F32)


def rms(flat, gain):
    power = jnp.mean(flat * flat, axis=-1, keepdims=True)
    return flat * lax.rsqrt(power + eps) * gain


def gelu(h):
    bent = jnp.tanh(h * (0.7978845608028654 + 0.035677408136300125 * (h * h)))
    half = 0.5 * h
    return half + half * bent


def halves_first(weight, axis_rows):
    grouped = weight.reshape(32, 2, 8, axis_rows).swapaxes(0, 1)
    return grouped.reshape(2, 256, axis_rows).astype(BF16)


def div(n, d):
    return n // d if isinstance(n, int) else lax.div(n, jnp.int32(d))


def mod(n, d):
    return n % d if isinstance(n, int) else lax.rem(n, jnp.int32(d))


def place(x, z, y, core):
    return x * 2 + div(z, 4), mod(z, 4) * 8 + y * 2 + core


def kernel(
    stream_hbm, wv_hbm, wg_hbm, wo_hbm, within_hbm, across_hbm, ws_hbm, as_hbm,
    mix_hbm, final_hbm, up_hbm, down_hbm,
    result,
    stream, wv, wg, wo, within, across, ws, ascale, mix_gain, final_gain, up, down,
    wvt, wgt, wot, partial, wst, normed, gates,
    send1, recv1, send2, recv2, send3, recv3, flip1, flip2,
    in_sem, s1, r1, s2, r2, s3, r3,
):
    chan = lax.axis_index("chan")
    seq = lax.axis_index("seq")
    x, z = div(chan, 2), mod(chan, 2) * 4 + div(seq, 8)
    y, core = mod(div(seq, 2), 4), mod(seq, 2)
    zl, yc = div(seq, 8), mod(seq, 8)
    own = x * 8 + z

    def p_block(half, y_of, core_of):
        return 2 * mod(x + y_of + 2 * core_of + half, NX) + core_of

    def load(number, source, target):
        return pltpu.make_async_copy(source, target, in_sem.at[number])

    loads = [
        load(1, wv_hbm, wv), load(2, mix_hbm, mix_gain),
        load(3, wg_hbm, wg), load(4, within_hbm, within), load(5, ws_hbm, ws),
        load(6, across_hbm, across), load(7, as_hbm, ascale), load(8, wo_hbm, wo),
        load(9, final_hbm, final_gain), load(10, up_hbm, up), load(11, down_hbm, down),
    ]
    loads = dict(zip(range(1, 12), loads))
    for part in range(2):
        rows = pl.ds(8 * part, 8)
        loads[12 + part] = load(12 + part, stream_hbm.at[rows], stream.at[rows])
    for number in (1, 12, 13, 2, 3, 4, 5, 6, 7, 8, 9, 10, 11):
        loads[number].start()

    barrier = pltpu.get_barrier_semaphore()

    def greet(x_of, z_of, y_of, core_of):
        pl.semaphore_signal(
            barrier, inc=1, device_id=place(x_of, z_of, y_of, core_of), device_id_type=MESH
        )

    @pl.loop(1, NX * NZ)
    def _(i):
        greet(mod(x + div(i, NZ), NX), mod(z + mod(i, NZ), NZ), y, core)

    @pl.loop(1, NY * NC)
    def _(i):
        greet(x, z, mod(y + div(i, NC), NY), mod(core + mod(i, NC), NC))


    for number in (1, 2):
        loads[number].wait()
    wvt[...] = halves_first(wv[...].astype(F32).T, 512)
    gain = mix_gain[...].astype(F32).reshape(1, 512)

    def values(half, pair, tokens):
        found = dot(wvt[half], tokens, LAST)
        split = [found[:, :128].reshape(32, 8, 128), found[:, 128:].reshape(32, 8, 128)]
        send1[half, :, pair] = jnp.concatenate(split, axis=1).astype(BF16)

    def send_values(half, block):
        rows = pl.ds(4 * block, 4)
        pltpu.make_async_copy(
            send1.at[half, own, rows], recv1.at[half, block, chan, zl], r1.at[half, block]
        ).start()

        @pl.loop(1, NX * NZ)
        def _(i):
            x_of, z_of = mod(x + div(i, NZ), NX), mod(z + mod(i, NZ), NZ)
            pltpu.make_async_remote_copy(
                send1.at[half, x_of * 8 + z_of, rows], recv1.at[half, block, chan, zl],
                s1.at[half], r1.at[half, block],
                device_id=place(x_of, z_of, y, core), device_id_type=MESH,
            ).start()

    for block in range(2):
        loads[12 + block].wait()

        @pl.loop(4 * block, 4 * block + 4)
        def _(pair):
            flat = stream[pl.ds(2 * pair, 2)].reshape(256, 512).astype(F32)
            tokens = rms(flat, gain).astype(BF16)
            normed[pair] = tokens
            values(0, pair, tokens)

        if block == 0:
            pl.semaphore_wait(barrier, NX * NZ - 1 + NY * NC - 1)
        send_values(0, block)

    for block in range(2):
        @pl.loop(4 * block, 4 * block + 4)
        def _(pair):
            values(1, pair, normed[pair])

        send_values(1, block)

    loads[3].wait()
    wgt[...] = halves_first(wg[...].astype(F32).T, 512)

    @pl.loop(0, 8)
    def _(pair):
        for half in range(2):
            found = dot(wgt[half], normed[pair], LAST).astype(BF16)
            gates[half, 2 * pair] = found[:, :128]
            gates[half, 2 * pair + 1] = found[:, 128:]

    loads[8].wait()
    wot[...] = halves_first(wo[...].astype(F32), 512)

    for number in (4, 5, 6, 7, 9, 10, 11):
        loads[number].wait()
    lower = lax.broadcasted_iota(jnp.int32, (256, 256), 0) >= lax.broadcasted_iota(jnp.int32, (256, 256), 1)
    for n in range(4):
        edge = pl.ds(256 * n, 256)
        within[edge, edge] = jnp.where(lower, within[edge, edge].astype(F32), 0.0).astype(BF16)
    for n in range(2):
        edge = pl.ds(256 * n, 256)
        across[edge, edge] = jnp.where(lower, across[edge, edge].astype(F32), 0.0).astype(BF16)
    old = lax.broadcasted_iota(jnp.int32, (256, 256), 0)
    new = lax.broadcasted_iota(jnp.int32, (256, 256), 1)
    moved = (old & 119) + ((old >> 3) & 1) * 128 + (old >> 7) * 8
    swap = (moved == new).astype(F32).astype(BF16)
    for n in range(2):
        edge = pl.ds(256 * n, 256)
        across[:, edge] = dot(across[:, edge], swap).astype(BF16)
    picked = lax.broadcasted_iota(jnp.int32, (16, 64), 1) == 16 * zl + lax.broadcasted_iota(jnp.int32, (16, 64), 0)
    wst[...] = dot(picked.astype(F32).astype(BF16), ws[...])

    def middle_of(half, block):
        arrived = recv1.at[half, block]
        pltpu.make_async_copy(arrived, arrived, r1.at[half, block]).wait()
        for n in range(4):
            blocks = [recv1[half, block, k].reshape(256, 128) for k in range(2 * n + 2)]
            found = dot(
                jnp.concatenate(blocks, axis=1), within[pl.ds(256 * n, 256), pl.ds(0, 256 * (n + 1))], LAST
            )
            scale = wst[pl.ds(8 * half, 8), pl.ds(256 * n, 256)]
            scaled = (found.reshape(32, 8, 256) * scale[None]).reshape(256, 256)
            for side in range(2):
                flip1[n, side] = scaled[:, 128 * side : 128 * side + 128]
            for side in range(2):
                for c in range(8):
                    column = flip1[n, side, pl.ds(c, 32, stride=8), :]
                    send2[half, block, 2 * n + side, c] = column.astype(BF16).reshape(2, 16, 128)
        pltpu.make_async_copy(
            send2.at[half, block, p_block(half, y, core)], recv2.at[half, block, yc], r2.at[half]
        ).start()

        @pl.loop(1, NY * NC)
        def _(i):
            y_of, core_of = mod(y + div(i, NC), NY), mod(core + mod(i, NC), NC)
            pltpu.make_async_remote_copy(
                send2.at[half, block, p_block(half, y_of, core_of)], recv2.at[half, block, yc],
                s2.at[half], r2.at[half],
                device_id=place(x, z, y_of, core_of), device_id_type=MESH,
            ).start()

    def across_of(half):
        pltpu.make_async_copy(recv2.at[half], recv2.at[half], r2.at[half]).wait()
        for c in range(0, 8, 2):
            both = jnp.concatenate(
                [
                    jnp.concatenate([
                            recv2[half, block, :, one, k].reshape(128, 128)
                            for k in range(2)
                            for block in range(2)
                        ], axis=0)
                    for one in (c, c + 1)
                ],
                axis=1,
            )
            row = lax.broadcasted_iota(jnp.int32, (64, 256), 0)
            wanted = 16 * zl + 8 * half + c + lax.broadcasted_iota(jnp.int32, (64, 256), 1) // 128
            spread = (row == wanted).astype(F32).astype(BF16)
            for n in range(2):
                rows = pl.ds(256 * n, 256)
                found = dot(across[rows, pl.ds(0, 256 * (n + 1))], both[: 256 * (n + 1)])
                found = found * dot(ascale[:, rows], spread, FIRST)
                for side in range(2):
                    flip2[pl.ds(2048 * n + c + side, 256, stride=8), :] = found[:, 128 * side : 128 * side + 128]

        @pl.loop(0, 32)
        def _(block):
            start = pl.multiple_of(block * 128, 128)
            send3[half, block] = flip2[pl.ds(start, 128), :].reshape(8, 16, 128).astype(BF16)

    def send_mixed(half, first, count, sem):
        block = p_block(half, y, core)
        rows = pl.ds(first, count)

        def remote(i):
            zl_of, yc_of = mod(zl + mod(i, 4), 4), mod(yc + div(i, 4), 8)
            seq_of = zl_of * 8 + yc_of
            pltpu.make_async_remote_copy(
                send3.at[half, seq_of, rows], recv3.at[half, own, rows],
                s3.at[sem], r3.at[sem], device_id=(block, seq_of), device_id_type=MESH,
            ).start()

        @pl.when(block == chan)
        def _():
            pltpu.make_async_copy(
                send3.at[half, seq, rows], recv3.at[half, own, rows], r3.at[sem]
            ).start()

        @pl.when(block != chan)
        def _():
            remote(0)

        @pl.loop(1, 32)
        def _(i):
            remote(i)

    middle_of(0, 0)
    middle_of(0, 1)
    across_of(0)
    send_mixed(0, 0, 8, PARTS)
    middle_of(1, 0)
    middle_of(1, 1)
    across_of(1)
    for part in range(PARTS):
        send_mixed(1, PP * part, PP, part)

    pltpu.make_async_copy(recv3.at[0], recv3.at[0], r3.at[PARTS]).wait()

    def projected(half, pair):
        mixed = recv3[half, :, pair].astype(F32)
        gated = [
            (mixed[:, 8 * one : 8 * one + 8].reshape(256, 128) * gates[half, 2 * pair + one].astype(F32)).astype(BF16)
            for one in range(2)
        ]
        return dot(jnp.concatenate(gated, axis=1), wot[half], FIRST)

    @pl.loop(0, 8)
    def _(pair):
        flat = stream[pl.ds(2 * pair, 2)].reshape(256, 512).astype(F32)
        partial[pair] = flat + projected(0, pair)

    gain2 = final_gain[...].astype(F32).reshape(1, 512)
    for part in range(PARTS):
        arrived = recv3.at[1, :, pl.ds(PP * part, PP)]
        pltpu.make_async_copy(arrived, arrived, r3.at[part]).wait()
        pairs = range(PP * part, PP * part + PP)
        middle = jnp.concatenate([partial[pair] + projected(1, pair) for pair in pairs], axis=0)
        middle = middle.astype(BF16).astype(F32)
        renormed = rms(middle, gain2).astype(BF16)
        outer = []
        for k in range(4):
            inner = gelu(dot(renormed[:, 128 * k : 128 * k + 128], up[k]).astype(GT)).astype(BF16)
            outer.append(dot(inner, down[k]))
        total = (middle + jnp.concatenate(outer, axis=1)).astype(BF16)
        result[pl.ds(2 * PP * part, 2 * PP)] = total.reshape(2 * PP, 128, 512)

    for half in range(2):
        sent = send1.at[half, pl.ds(0, 31)]
        pltpu.make_async_copy(sent, sent, s1.at[half]).wait()
        sent = send2.at[half, :, pl.ds(0, 7)]
        pltpu.make_async_copy(sent, sent, s2.at[half]).wait()
    for sem in range(PARTS + 1):
        rows = pl.ds(0, 8) if sem == PARTS else pl.ds(PP * sem, PP)
        half = 0 if sem == PARTS else 1
        rest = send3.at[half, pl.ds(1, 31), rows]
        pltpu.make_async_copy(rest, rest, s3.at[sem]).wait()

        @pl.when(p_block(half, y, core) != chan)
        def _():
            one = send3.at[half, 0, rows]
            pltpu.make_async_copy(one, one, s3.at[sem]).wait()


def body(
    stream, weight_value, weight_gate, weight_out, within_factor, across_factor,
    within_scale, across_scale, mix_gain, final_gain, block_up, block_down,
):
    args = (
        stream, weight_value, weight_gate, weight_out, within_factor, across_factor,
        within_scale.T, across_scale.T, mix_gain, final_gain,
        block_up, block_down,
    )
    anywhere = pl.BlockSpec(memory_space=pl.ANY)
    return pl.pallas_call(
        kernel,
        out_shape=pltpu.VMEM(stream.shape, BF16),
        in_specs=[anywhere] * len(args),
        out_specs=pl.BlockSpec(memory_space=pltpu.VMEM),
        scratch_shapes=[pltpu.VMEM(a.shape, BF16) for a in args] + [
            pltpu.VMEM((2, 256, 512), BF16),
            pltpu.VMEM((2, 256, 512), BF16),
            pltpu.VMEM((2, 256, 512), BF16),
            pltpu.VMEM((8, 256, 512), F32),
            pltpu.VMEM((16, 1024), F32),
            pltpu.VMEM((8, 256, 512), BF16),
            pltpu.VMEM((2, 16, 256, 128), BF16),
            pltpu.VMEM((2, 32, 8, 16, 128), BF16),
            pltpu.VMEM((2, 2, 8, 4, 4, 16, 128), BF16),
            pltpu.VMEM((2, 2, 8, 8, 2, 16, 128), BF16),
            pltpu.VMEM((2, 2, 8, 8, 2, 16, 128), BF16),
            pltpu.VMEM((2, 32, 8, 16, 128), BF16),
            pltpu.VMEM((2, 32, 8, 16, 128), BF16),
            pltpu.VMEM((4, 2, 256, 128), F32),
            pltpu.VMEM((4096, 128), F32),
            pltpu.SemaphoreType.DMA((14,)),
            pltpu.SemaphoreType.DMA((2,)),
            pltpu.SemaphoreType.DMA((2, 2)),
            pltpu.SemaphoreType.DMA((2,)),
            pltpu.SemaphoreType.DMA((2,)),
            pltpu.SemaphoreType.DMA((PARTS + 1,)),
            pltpu.SemaphoreType.DMA((PARTS + 1,)),
        ],
        compiler_params=pltpu.CompilerParams(
            collective_id=0, has_side_effects=True, vmem_limit_bytes=56 * 2**20
        ),
        cost_estimate=pl.CostEstimate(
            flops=9 * 10**9, bytes_accessed=12 * 2**20, transcendentals=2**22
        ),
        name="mixer",
    )(*args)


def solution(mesh):
    placed = (
        P("seq", "chan", None), P(), P(), P(), P(), P(), P(None, "chan"), P(None, "chan"),
        P(), P(), P(), P(),
    )
    return jax.shard_map(
        body, mesh=mesh, in_specs=placed, out_specs=P("seq", "chan", None), check_vma=False
    )
```
